128 devices in a mesh: grp: 8 (over x_hi, z), mem: 16 (over x_lo, y, core).
Axes of the slice: x: 4 (x_hi: 2, x_lo: 2; x = x_hi * 2 + x_lo), y: 4, z: 4, core: 2. Of those that a mesh axis runs over, the one named last changes fastest.
Arguments:
- tokens: bfloat16 [4096, 8192], P('grp', 'mem'), may hold values from -6 to 6
- base_weight: bfloat16 [8192, 14336], P(None, 'mem'), may hold values from -0.0625 to 0.0625
- adapt_down: bfloat16 [32, 8192, 64], P('grp', 'mem'), may hold values from -0.0625 to 0.0625
- adapt_up: bfloat16 [32, 64, 14336], P('grp', None, 'mem'), may hold values from -0.046875 to 0.046875
- cotangent: bfloat16 [4096, 14336], P('grp', 'mem'), may hold values from -6 to 6
- tenant: int32 [32], replicated, may hold values from 0 to 31
- adapter_slot: int32 [32], replicated, may hold values from 0 to 31, each once
Outputs:
- mixed: bfloat16 [4096, 14336], P('grp', 'mem')
- token_gradient: bfloat16 [4096, 8192], P('grp', 'mem')
- down_grad: bfloat16 [32, 8192, 64], P('grp', 'mem')
- up_grad: bfloat16 [32, 64, 14336], P('grp', None, 'mem')
The draws below stay inside these ranges and needn't reach their ends.
Inputs may be any that keep to these rules, and one draw needn't show every extreme that they name: `adapter_slot`: each slot is held by exactly one adapter.
All inputs are finite; a program needn't handle non-finite values.
Results may differ from the reference program's by a relative error of at most 0.02.
Values may be sent and summed in bfloat16 or wider, within the bound.
No kernel may reach another device: no remote copies, remote signals or barrier semaphores. Data moves between devices by JAX's collectives and lax.ppermute only.
A program may use at most 128 MiB of HBM per device.

```python
import math
import jax
import jax.numpy as jnp
import numpy as np
from jax import lax

D = 8192
FW = 14336
R = 64
NAD = 32
TENANT_TOKENS = 128
NBLK = 32
TOKENS = 4096
N_MEM = 16


def set_ends(entries, stream_key, low, top_value):
    longest = entries.shape.index(max(entries.shape))
    spots = []
    for shift in (0, 1):
        where = [jax.random.randint(jax.random.fold_in(stream_key, axis), (), 0, length) for axis, length in enumerate(entries.shape)]
        where[longest] = (where[longest] + shift) % entries.shape[longest]
        spots.append(tuple(where))
    return entries.at[spots[0]].set(low).at[spots[1]].set(top_value)


def steps_of(key, dims, cuts, low, largest):
    def one(dim, parts):
        heights = jax.random.uniform(jax.random.fold_in(jax.random.fold_in(key, 6), dim), (parts,), jnp.float32, low / len(cuts), largest / len(cuts))
        return jnp.repeat(jnp.exp(heights), dims[dim] // parts).reshape((-1,) + (1,) * (len(dims) - dim - 1))

    loudness = one(*cuts[0])
    for cut in cuts[1:]:
        loudness = loudness * one(*cut)
    return loudness


def cumulative_ranks(amount, skew):
    portions = [(1 << 20) // math.isqrt(grade ** skew) + 1 for grade in range(1, amount + 1)]
    spread = 1 + sum(portions) // (1 << 30)
    return np.cumsum(np.array([max(1, weight // spread) for weight in portions]))


def ranked_ids(own_key, shape, number_of, skew):
    table = cumulative_ranks(number_of, skew)
    pick = jax.random.randint(jax.random.fold_in(own_key, 1), shape, 0, int(table[number_of - 1]))
    standing = jnp.searchsorted(jnp.asarray(table, jnp.int32), pick, side="right")
    return jax.random.permutation(jax.random.fold_in(own_key, 2), number_of)[standing].astype(jnp.int32)


def gaussian(key, extent, deviation, limit, pieces=(), kind=jnp.bfloat16):
    factor_of = steps_of(key, extent, pieces, -0.22, 0.18) if pieces else 1.0
    array = jax.random.normal(key, extent, jnp.float32) * deviation * factor_of
    return jnp.minimum(jnp.maximum(array, -limit), limit).astype(kind)


def setup_inputs(seed: int = 0) -> dict:
    key_list = jax.random.split(jax.random.key(seed), 8)
    tokens = gaussian(key_list[0], (TOKENS, D), 1.0, 6.0, ((0, 8), (1, 16)))
    base_weight = gaussian(key_list[1], (D, FW), D ** -0.5, 0.0625, ((1, 16),))
    adapt_down = gaussian(key_list[2], (NAD, D, R), D ** -0.5, 0.0625, ((0, 8), (1, 16)))
    adapt_up = gaussian(key_list[3], (NAD, R, FW), FW ** -0.5, 0.046875, ((0, 8), (2, 16)))
    cotangent = gaussian(key_list[4], (TOKENS, FW), 1.0, 6.0, ((0, 8), (1, 16)))
    tenant = set_ends(ranked_ids(key_list[5], (NBLK,), NAD, 2), jax.random.fold_in(key_list[5], 3), 0, NAD - 1).astype(jnp.int32)
    adapter_slot = jax.random.permutation(key_list[6], NAD).astype(jnp.int32)
    return dict(tokens=tokens, base_weight=base_weight, adapt_down=adapt_down, adapt_up=adapt_up, cotangent=cotangent, tenant=tenant, adapter_slot=adapter_slot)


adapter_scale = 8.0


def reference(tokens, base_weight, adapt_down, adapt_up, cotangent, tenant, adapter_slot):
    block_slots = adapter_slot[tenant].astype(jnp.int32)
    down_blocks = adapt_down[block_slots].astype(jnp.float32)
    up_blocks = adapt_up[block_slots].astype(jnp.float32)
    token_blocks = tokens.reshape(NBLK, TENANT_TOKENS, D).astype(jnp.float32)
    cot_blocks = cotangent.reshape(NBLK, TENANT_TOKENS, FW).astype(jnp.float32)
    low_rank = jnp.einsum("nbd,ndr->nbr", token_blocks, down_blocks).astype(jnp.bfloat16)
    base_output = jnp.dot(tokens, base_weight, preferred_element_type=jnp.float32)
    lowrank_output = jnp.einsum("nbr,nrf->nbf", low_rank.astype(jnp.float32), up_blocks).reshape(TOKENS, FW)
    mixed = (base_output + adapter_scale * lowrank_output).astype(jnp.bfloat16)
    cot_rank = jnp.einsum("nbf,nrf->nbr", cot_blocks, up_blocks).astype(jnp.bfloat16)
    shard_width = FW // N_MEM

    def accumulate(running, member):
        offset = (member * shard_width).astype(jnp.int32)
        cot_part = lax.dynamic_slice_in_dim(cotangent, offset, shard_width, 1)
        weight_part = lax.dynamic_slice_in_dim(base_weight, offset, shard_width, 1)
        partial_term = lax.dot_general(cot_part, weight_part, (((1,), (1,)), ((), ())), preferred_element_type=jnp.float32)
        rounded = lax.optimization_barrier(partial_term.astype(jnp.bfloat16))
        return running + rounded.astype(jnp.float32), None

    summed_output, _ = lax.scan(accumulate, jnp.zeros((TOKENS, D), jnp.float32), jnp.arange(N_MEM, dtype=jnp.int32))
    lowrank_backward = jnp.einsum("nbr,ndr->nbd", cot_rank.astype(jnp.float32), down_blocks).reshape(TOKENS, D)
    token_gradient = (summed_output + adapter_scale * lowrank_backward).astype(jnp.bfloat16)
    scaling_factor = adapter_scale / TENANT_TOKENS
    grad_down_blocks = jnp.einsum("nbd,nbr->ndr", token_blocks, cot_rank.astype(jnp.float32)) * scaling_factor
    grad_up_blocks = jnp.einsum("nbr,nbf->nrf", low_rank.astype(jnp.float32), cot_blocks) * scaling_factor
    down_grad = jnp.zeros((NAD, D, R), jnp.float32).at[block_slots].add(grad_down_blocks).astype(jnp.bfloat16)
    up_grad = jnp.zeros((NAD, R, FW), jnp.float32).at[block_slots].add(grad_up_blocks).astype(jnp.bfloat16)
    return (mixed, token_gradient, down_grad, up_grad)
```

```python
import functools

import jax
import jax.numpy as jnp
from jax import lax
from jax.experimental import pallas as pl
from jax.experimental.pallas import tpu as pltpu
from jax.sharding import PartitionSpec as P

SCALE = 8.0
GRP, XL, YY, CORES = 8, 2, 4, 2
BLK = 4
F32, BF16 = jnp.float32, jnp.bfloat16
VMEM = pl.BlockSpec(memory_space=pltpu.VMEM)
SMEM = pl.BlockSpec(memory_space=pltpu.SMEM)
ANY = pl.BlockSpec(memory_space=pl.ANY)
LIMIT = 50 * 1024 * 1024


def mem_perm(move):
    pairs = []
    for x in range(XL):
        for y in range(YY):
            for c in range(CORES):
                tx, ty, tc = move(x, y, c)
                pairs.append(((x * YY + y) * CORES + c, (tx * YY + ty % YY) * CORES + tc))
    return pairs


def way(c):
    return 1 - 2 * c


MOVES = {
    "core": mem_perm(lambda x, y, c: (x, y, 1 - c)),
    "x": mem_perm(lambda x, y, c: (1 - x, y, c)),
    "fwd": mem_perm(lambda x, y, c: (x, y + way(c), c)),
    "back": mem_perm(lambda x, y, c: (x, y - way(c), c)),
    "far": mem_perm(lambda x, y, c: (x, y + 2, c)),
}


def send(value, move):
    return lax.ppermute(value, "mem", MOVES[move])


def exchange(pieces):
    return [pieces[0]] + [
        lax.ppermute(pieces[i], "grp", [(g, g ^ i) for g in range(GRP)]) for i in (2, 6, 4, 7, 5, 3, 1)
    ]


def ordered(received):
    order = (0, 2, 6, 4, 7, 5, 3, 1)
    return [received[order.index(i)] for i in range(GRP)]


def params(**kw):
    return pltpu.CompilerParams(vmem_limit_bytes=LIMIT, **kw)


def cut_kernel(group, down, up, *outs):
    width = down.shape[-1]
    for i in range(GRP):
        piece = group[0] ^ i
        for b in range(BLK):
            outs[i][b, :, :width] = down[b, piece]
            outs[i][b, :, width:] = up[b, piece]


def pick_kernel(index, *refs):
    ins, outs, held = refs[:GRP], refs[GRP : 2 * GRP], refs[2 * GRP]
    for i in range(GRP):
        held[BLK * i : BLK * (i + 1)] = ins[i][...]
    for i in range(GRP):
        for b in range(BLK):
            outs[i][b] = held[index[BLK * i + b]]


def rank_kernel(tokens, cot, *refs):
    ins, adapters, part = refs[:GRP], refs[GRP], refs[GRP + 1]
    width = tokens.shape[1]
    rows = tokens.shape[0] // BLK
    rank = adapters.shape[1]
    for b in range(BLK):
        whole = jnp.concatenate([ins[i][b].astype(F32) for i in range(GRP)], axis=0).astype(BF16)
        adapters[b] = whole
        span = slice(b * rows, (b + 1) * rows)
        dims = (((1,), (1,)), ((), ()))
        part[span, :rank] = lax.dot_general(tokens[span, :], whole[:, :width], dims, preferred_element_type=F32)
        part[span, rank:] = lax.dot_general(cot[span, :], whole[:, width:], dims, preferred_element_type=F32)


def grad_kernel(tokens, cot, ranks, *outs):
    width = tokens.shape[1]
    rows = tokens.shape[0] // BLK
    rank = ranks.shape[1] // 2
    piece = rank // GRP
    factor = SCALE / rows
    dims = (((0,), (0,)), ((), ()))
    for b in range(BLK):
        span = slice(b * rows, (b + 1) * rows)
        both = ranks[span, :]
        low, back = both[:, :rank], both[:, rank:]
        down = lax.dot_general(back, tokens[span, :], dims, preferred_element_type=F32) * factor
        up = lax.dot_general(low, cot[span, :], dims, preferred_element_type=F32) * factor
        for i in range(GRP):
            part = slice(i * piece, (i + 1) * piece)
            outs[i][b, :, :width] = down[part].astype(BF16)
            outs[i][b, :, width:] = up[part].astype(BF16)


def total_kernel(index, *refs):
    ins, outs, total = refs[:GRP], refs[GRP : 2 * GRP], refs[2 * GRP]
    total[...] = jnp.zeros_like(total)
    for i in range(GRP):
        for b in range(BLK):
            slot = index[BLK * i + b]
            total[slot] = total[slot] + ins[i][b].astype(F32)
    for i in range(GRP):
        outs[i][...] = total[BLK * i : BLK * (i + 1)].astype(BF16)


def join_kernel(group, *refs):
    ins, down, up = refs[:GRP], refs[GRP], refs[GRP + 1]
    width = down.shape[-1]
    for i in range(GRP):
        piece = group[0] ^ i
        for b in range(BLK):
            down[b, piece] = ins[i][b, :, :width]
            up[b, piece] = ins[i][b, :, width:]


def copy_kernel(order, source, out):
    out[...] = source[...]


def back_kernel(order, cot, cot_pair, own, pair, *outs):
    i = pl.program_id(0)
    dims = (((1,), (1,)), ((), ()))
    value = lax.dot_general(cot[...], own[0], dims, preferred_element_type=F32)
    value += lax.dot_general(cot_pair[...], pair[0], dims, preferred_element_type=F32)
    value = value.astype(BF16)
    for k in range(len(outs)):

        @pl.when(i == k)
        def _():
            outs[k][...] = value


def ahead_kernel(count, first, order, *refs):
    shards, refs = refs[:count], refs[count:]
    if first:
        own, pair, out_own, out_pair, held, sems = refs
    else:
        own, pair, start_own, start_pair, out_own, out_pair, held, sems = refs
    i = pl.program_id(0)
    copies = [pltpu.make_async_copy(shards[k], held.at[k], sems.at[k]) for k in range(count)]

    @pl.when(i == 0)
    def _():
        for copy in copies:
            copy.start()
        out_own[...] = jnp.zeros_like(out_own) if first else start_own[...]
        out_pair[...] = jnp.zeros_like(out_pair) if first else start_pair[...]

    for k in range(count):

        @pl.when(i == k)
        def _():
            copies[k].wait()

    shard = held[i]
    out_own[...] += jnp.dot(shard, own[0], preferred_element_type=F32)
    out_pair[...] += jnp.dot(shard, pair[0], preferred_element_type=F32)


def ahead(shards, weight, pair, order, start):
    count = len(shards)
    rows, depth = shards[0].shape
    wide = weight.shape[2]
    first = start is None
    total = pl.BlockSpec((rows, wide), lambda i, order: (0, 0))
    block = (1, depth, wide)
    specs = [ANY] * count + [
        pl.BlockSpec(block, lambda i, order: (order[i], 0, 0)),
        pl.BlockSpec(block, lambda i, order: (i, 0, 0)),
    ]
    if not first:
        specs += [total, total]
    return pl.pallas_call(
        functools.partial(ahead_kernel, count, first),
        grid_spec=pltpu.PrefetchScalarGridSpec(
            num_scalar_prefetch=1,
            grid=(count,),
            in_specs=specs,
            out_specs=[total, total],
            scratch_shapes=[pltpu.VMEM((count, rows, depth), BF16), pltpu.SemaphoreType.DMA((count,))],
        ),
        out_shape=[jax.ShapeDtypeStruct((rows, wide), F32)] * 2,
        compiler_params=params(),
        cost_estimate=pl.CostEstimate(
            flops=4 * count * rows * depth * wide, bytes_accessed=4 * count * depth * wide, transcendentals=0
        ),
        name="ahead",
    )(order, *shards, weight, pair, *(() if first else start))


def take_blocks(weight, order):
    count = order.shape[0]
    block = (1,) + weight.shape[1:]
    return pl.pallas_call(
        copy_kernel,
        grid_spec=pltpu.PrefetchScalarGridSpec(
            num_scalar_prefetch=1,
            grid=(count,),
            in_specs=[pl.BlockSpec(block, lambda i, order: (order[i], 0, 0))],
            out_specs=pl.BlockSpec(block, lambda i, order: (i, 0, 0)),
        ),
        out_shape=jax.ShapeDtypeStruct((count,) + weight.shape[1:], BF16),
        compiler_params=params(),
        name="take_blocks",
    )(order, weight)


def backward(cot, cot_pair, weight, pair, order):
    count = order.shape[0]
    rows, wide = cot.shape
    depth = weight.shape[1]
    block = (1, depth, wide)
    whole = pl.BlockSpec((rows, wide), lambda i, order: (0, 0))
    return pl.pallas_call(
        back_kernel,
        grid_spec=pltpu.PrefetchScalarGridSpec(
            num_scalar_prefetch=1,
            grid=(count,),
            in_specs=[
                whole,
                whole,
                pl.BlockSpec(block, lambda i, order: (order[i], 0, 0)),
                pl.BlockSpec(block, lambda i, order: (i, 0, 0)),
            ],
            out_specs=[pl.BlockSpec((rows, depth), lambda i, order: (0, 0))] * count,
        ),
        out_shape=[jax.ShapeDtypeStruct((rows, depth), BF16)] * count,
        compiler_params=params(),
        cost_estimate=pl.CostEstimate(
            flops=4 * count * rows * depth * wide, bytes_accessed=4 * count * depth * wide, transcendentals=0
        ),
        name="backward",
    )(order, cot, cot_pair, weight, pair)


def plus(*terms):
    total = terms[0].astype(F32)
    for term in terms[1:]:
        total = total + term.astype(F32)
    return total


def shards(tokens, base_weight, adapt_down, adapt_up, cotangent, tenant, adapter_slot):
    group = lax.axis_index("grp").astype(jnp.int32)
    member = lax.axis_index("mem").astype(jnp.int32)
    core, y, x = member % 2, (member // 2) % YY, member // (2 * YY)
    rows, feats = tokens.shape
    hidden = cotangent.shape[1]
    per_group, _, rank = adapt_down.shape
    piece = rank // GRP
    groups = jnp.arange(GRP, dtype=jnp.int32) ^ group

    match = tenant[:, None] == jnp.arange(adapter_slot.shape[0], dtype=jnp.int32)[None, :]
    slots = jnp.sum(jnp.where(match, adapter_slot[None, :], 0), axis=1)
    blocks = (groups[:, None] * BLK + jnp.arange(BLK, dtype=jnp.int32)[None, :]).reshape(-1)
    mine = jnp.sum(
        jnp.where(blocks[:, None] == jnp.arange(slots.shape[0], dtype=jnp.int32)[None, :], slots[None, :], 0), axis=1
    )
    index = ((mine // per_group) ^ group) * per_group + mine % per_group

    def block_order(c):
        d = 1 - 2 * c
        steps = ((0, 0), (1, 0), (0, -d), (0, d), (1, -d), (1, d), (0, 2), (1, 2))
        return jnp.stack([((x ^ dx) * YY + (y + dy + YY) % YY) * 2 + c for dx, dy in steps]).astype(jnp.int32)

    order, pair_order = block_order(core), block_order(1 - core)

    piece_shape = jax.ShapeDtypeStruct((per_group, piece, feats + hidden), BF16)
    down_t = jnp.swapaxes(adapt_down, 1, 2)
    group1 = group[None]

    cut = pl.pallas_call(
        cut_kernel,
        in_specs=[SMEM, VMEM, VMEM],
        out_specs=[VMEM] * GRP,
        out_shape=[piece_shape] * GRP,
        compiler_params=params(),
        name="cut",
    )(group1, down_t.reshape(per_group, GRP, piece, feats), adapt_up.reshape(per_group, GRP, piece, hidden))
    got = ordered(exchange(cut))

    t_x = send(tokens, "x")
    t_f = send(tokens, "fwd")
    t_b = send(tokens, "back")
    cot_pair = send(cotangent, "core")

    weight = base_weight.reshape(2 * XL * YY, feats, hidden)
    half = order.shape[0] // 2
    pair_w = [send(take_blocks(weight, pair_order[k : k + half]), "core") for k in (0, half)]

    t_ff = send(t_f, "fwd")
    t_xf = send(t_x, "fwd")
    t_xb = send(t_x, "back")
    t_xff = send(t_ff, "x")

    picked = pl.pallas_call(
        pick_kernel,
        in_specs=[SMEM] + [VMEM] * GRP,
        out_specs=[VMEM] * GRP,
        out_shape=[piece_shape] * GRP,
        scratch_shapes=[pltpu.VMEM((GRP * per_group, piece, feats + hidden), BF16)],
        compiler_params=params(),
        name="pick",
    )(index, *got)
    own_adapters = ordered(exchange(picked))
    adapters, part = pl.pallas_call(
        rank_kernel,
        in_specs=[VMEM] * (2 + GRP),
        out_specs=[VMEM] * 2,
        out_shape=[
            jax.ShapeDtypeStruct((BLK, rank, feats + hidden), BF16),
            jax.ShapeDtypeStruct((rows, 2 * rank), F32),
        ],
        compiler_params=params(),
        name="rank",
    )(tokens, cotangent, *own_adapters)

    parts = []
    for k in (0, half):
        parts += backward(cotangent, cot_pair, weight, pair_w[k // half], order[k : k + half])

    middle = rows // 2
    keep = jnp.where(core == 0, part[:middle], part[middle:])
    give = jnp.where(core == 0, part[middle:], part[:middle])
    chip = (keep + send(give, "core")).astype(BF16)
    two = plus(chip, send(chip, "x")).astype(BF16)
    half_sum = plus(two, send(two, "fwd"), send(two, "back"), send(two, "far")).astype(BF16)
    other = send(half_sum, "core")
    ranks = jnp.concatenate(
        [jnp.where(core == 0, half_sum, other), jnp.where(core == 0, other, half_sum)], axis=0
    )

    grads = pl.pallas_call(
        grad_kernel,
        in_specs=[VMEM] * 3,
        out_specs=[VMEM] * GRP,
        out_shape=[piece_shape] * GRP,
        compiler_params=params(),
        name="grads",
    )(tokens, cotangent, ranks)
    got = ordered(exchange(grads))
    totals = pl.pallas_call(
        total_kernel,
        in_specs=[SMEM] + [VMEM] * GRP,
        out_specs=[VMEM] * GRP,
        out_shape=[piece_shape] * GRP,
        scratch_shapes=[pltpu.VMEM((GRP * per_group, piece, feats + hidden), F32)],
        compiler_params=params(),
        name="total",
    )(index, *got)
    final = ordered(exchange(totals))
    down_grad, up_grad = pl.pallas_call(
        join_kernel,
        in_specs=[SMEM] + [VMEM] * GRP,
        out_specs=[VMEM] * 2,
        out_shape=[
            jax.ShapeDtypeStruct((per_group, GRP, piece, feats), BF16),
            jax.ShapeDtypeStruct((per_group, GRP, piece, hidden), BF16),
        ],
        compiler_params=params(),
        name="join",
    )(group1, *final)
    down_grad = jnp.swapaxes(down_grad.reshape(per_group, rank, feats), 1, 2)
    up_grad = up_grad.reshape(per_group, rank, hidden)

    g00, g10, g0b, g0f, g1b, g1f, g02, g12 = parts
    r_12 = send(g12, "x")
    r_1b = send(g1b, "back")
    r_1f = send(g1f, "fwd")
    r_0f = send(g0f, "fwd")
    r_02 = send(plus(g02, r_12).astype(BF16), "back")
    r_10 = send(plus(g10, r_1b, r_1f).astype(BF16), "x")
    r_0b = send(plus(g0b, r_02).astype(BF16), "back")
    cot_rank = ranks[:, rank:].reshape(BLK, rows // BLK, rank)
    low_rank = ranks[:, :rank].reshape(BLK, rows // BLK, rank)
    low_back = jnp.einsum("kbr,krd->kbd", cot_rank, adapters[:, :, :feats], preferred_element_type=F32)
    token_gradient = (plus(g00, r_0f, r_10, r_0b) + SCALE * low_back.reshape(rows, feats)).astype(BF16)

    first = ahead([tokens, t_x, t_f, t_b], weight, pair_w[0], order[:half], None)
    own_sum, pair_sum = ahead([t_xf, t_xb, t_ff, t_xff], weight, pair_w[1], order[half:], first)
    from_pair = send(pair_sum.astype(BF16), "core")
    low_out = jnp.einsum("kbr,krf->kbf", low_rank, adapters[:, :, feats:], preferred_element_type=F32)
    mixed = (own_sum + from_pair.astype(F32) + SCALE * low_out.reshape(rows, hidden)).astype(BF16)
    return mixed, token_gradient, down_grad, up_grad


def solution(mesh):
    in_specs = (
        P("grp", "mem"),
        P(None, "mem"),
        P("grp", "mem", None),
        P("grp", None, "mem"),
        P("grp", "mem"),
        P(),
        P(),
    )
    out_specs = (P("grp", "mem"), P("grp", "mem"), P("grp", "mem", None), P("grp", None, "mem"))
    return jax.shard_map(shards, mesh=mesh, in_specs=in_specs, out_specs=out_specs, check_vma=False)
```

```python
import functools

import jax
import jax.numpy as jnp
from jax import lax
from jax.experimental import pallas as pl
from jax.experimental.pallas import tpu as pltpu
from jax.sharding import PartitionSpec as P

SCALE = 8.0
GRP, XL, YY, CORES = 8, 2, 4, 2
BLK = 4
F32, BF16 = jnp.float32, jnp.bfloat16
VMEM = pl.BlockSpec(memory_space=pltpu.VMEM)
SMEM = pl.BlockSpec(memory_space=pltpu.SMEM)
HBM = pl.BlockSpec(memory_space=pltpu.HBM)
ANY = pl.BlockSpec(memory_space=pl.ANY)
WIDE = 56
COST = pl.CostEstimate(flops=1, bytes_accessed=1, transcendentals=0)
NT = (((1,), (1,)), ((), ()))
TN = (((0,), (0,)), ((), ()))


def mem_perm(move):
    pairs = []
    for x in range(XL):
        for y in range(YY):
            for c in range(CORES):
                tx, ty, tc = move(x, y, c)
                pairs.append(((x * YY + y) * CORES + c, (tx * YY + ty % YY) * CORES + tc))
    return pairs


def way(c):
    return 1 - 2 * c


MOVES = {
    "core": mem_perm(lambda x, y, c: (x, y, 1 - c)),
    "x": mem_perm(lambda x, y, c: (1 - x, y, c)),
    "fwd": mem_perm(lambda x, y, c: (x, y + way(c), c)),
    "back": mem_perm(lambda x, y, c: (x, y - way(c), c)),
    "far": mem_perm(lambda x, y, c: (x, y + 2, c)),
}


def send(value, move, name):
    with jax.named_scope(name):
        return lax.ppermute(value, "mem", MOVES[move])


def stay(value):
    return pltpu.with_memory_space_constraint(value, pltpu.HBM)


def exchange(pieces):
    return lax.all_to_all(pieces, "grp", 0, 0, tiled=True)


def params(mib):
    return pltpu.CompilerParams(vmem_limit_bytes=mib * 1024 * 1024)


def cut_kernel(down, up, out):
    width = down.shape[-1]
    out[:, 0, :, :width] = down[0]
    out[:, 0, :, width:] = up[0]


def pick_kernel(slots, got, out):
    for i in range(GRP):
        for b in range(BLK):
            slot = slots[BLK * i + b]
            out[i, b] = got[slot // BLK, slot % BLK]


def rank_kernel(tokens, cot, got, adapters, part):
    width = tokens.shape[1]
    rank = adapters.shape[1]
    whole = jnp.concatenate([got[i, 0].astype(F32) for i in range(GRP)], axis=0).astype(BF16)
    adapters[0] = whole
    part[:, :rank] = lax.dot_general(tokens[...], whole[:, :width], NT, preferred_element_type=F32)
    part[:, rank:] = lax.dot_general(cot[...], whole[:, width:], NT, preferred_element_type=F32)


def grad_kernel(tokens, cot, ranks, out):
    width = tokens.shape[1]
    rows = tokens.shape[0]
    rank = ranks.shape[1] // 2
    piece = rank // GRP
    factor = SCALE / rows
    both = ranks[...]
    down = lax.dot_general(both[:, rank:], tokens[...], TN, preferred_element_type=F32) * factor
    up = lax.dot_general(both[:, :rank], cot[...], TN, preferred_element_type=F32) * factor
    for i in range(GRP):
        part = slice(i * piece, (i + 1) * piece)
        out[i, 0, :, :width] = down[part].astype(BF16)
        out[i, 0, :, width:] = up[part].astype(BF16)


def total_kernel(slots, got, out, total):
    total[...] = jnp.zeros_like(total)
    for i in range(GRP):
        for b in range(BLK):
            slot = slots[BLK * i + b]
            total[slot] = total[slot] + got[i, b].astype(F32)
    for i in range(GRP):
        out[i] = total[BLK * i : BLK * (i + 1)].astype(BF16)


def join_kernel(got, down, up):
    width = down.shape[-1]
    down[0] = got[:, 0, :, :width]
    up[0] = got[:, 0, :, width:]


def back_kernel(count, order, cot, cot_pair, own, pair, *refs):
    outs, (ready, out_sems) = refs[:count], refs[count:]
    i = pl.program_id(0)
    copies = [pltpu.make_async_copy(ready.at[k % 2], outs[k], out_sems.at[k % 2]) for k in range(count)]
    for k in range(2, count):

        @pl.when(i == k)
        def _():
            copies[k - 2].wait()

    value = lax.dot_general(cot[...], own[0], NT, preferred_element_type=F32)
    value += lax.dot_general(cot_pair[...], pair[0], NT, preferred_element_type=F32)
    ready[lax.rem(i, 2)] = value.astype(BF16)
    for k in range(count):

        @pl.when(i == k)
        def _():
            copies[k].start()

    @pl.when(i == count - 1)
    def _():
        copies[-2].wait()
        copies[-1].wait()


def backward(cot, cot_pair, weight, pair, order):
    count = order.shape[0]
    rows, wide = cot.shape
    depth = weight.shape[1]
    whole = pl.BlockSpec((rows, wide), lambda i, order: (0, 0))
    block = pl.BlockSpec((1, depth, wide), lambda i, order: (order[i], 0, 0))
    return pl.pallas_call(
        functools.partial(back_kernel, count),
        grid_spec=pltpu.PrefetchScalarGridSpec(
            num_scalar_prefetch=1,
            grid=(count,),
            in_specs=[whole, whole, block, block],
            out_specs=[HBM] * count,
            scratch_shapes=[pltpu.VMEM((2, rows, depth), BF16), pltpu.SemaphoreType.DMA((2,))],
        ),
        out_shape=[pltpu.HBM((rows, depth), BF16)] * count,
        compiler_params=params(30),
        cost_estimate=COST,
        name="backward",
    )(order, cot, cot_pair, weight, pair)


def ahead_kernel(count, order, *refs):
    pieces, (own, pair, ranks, adapters, out, out_pair) = refs[:count], refs[count : count + 6]
    held, total, sems = refs[count + 6 :]
    i = pl.program_id(0)
    copies = [pltpu.make_async_copy(s, held.at[k], sems.at[k]) for k, s in enumerate(pieces)]

    @pl.when(i == 0)
    def _():
        for copy in copies:
            copy.start()
        rank = adapters.shape[1]
        rows = ranks.shape[0] // BLK
        width = adapters.shape[2] - out.shape[1]
        for b in range(BLK):
            span = slice(b * rows, (b + 1) * rows)
            out[span, :] = SCALE * jnp.dot(ranks[span, :rank], adapters[b, :, width:], preferred_element_type=F32)
        total[...] = jnp.zeros_like(total)

    for k in range(count):

        @pl.when(i == k)
        def _():
            copies[k].wait()

    out[...] += jnp.dot(held[i], own[0], preferred_element_type=F32)
    total[...] += jnp.dot(held[i], pair[0], preferred_element_type=F32)

    @pl.when(i == count - 1)
    def _():
        out_pair[...] = total[...].astype(BF16)


def ahead(pieces, weight, pair, ranks, adapters, order):
    count = len(pieces)
    rows, depth = pieces[0].shape
    wide = weight.shape[2]
    block = pl.BlockSpec((1, depth, wide), lambda i, order: (order[i], 0, 0))
    total = pl.BlockSpec((rows, wide), lambda i, order: (0, 0))
    return pl.pallas_call(
        functools.partial(ahead_kernel, count),
        grid_spec=pltpu.PrefetchScalarGridSpec(
            num_scalar_prefetch=1,
            grid=(count,),
            in_specs=[HBM] * count
            + [
                block,
                block,
                pl.BlockSpec(ranks.shape, lambda i, order: (0, 0)),
                pl.BlockSpec(adapters.shape, lambda i, order: (0, 0, 0)),
            ],
            out_specs=[total, total],
            scratch_shapes=[
                pltpu.VMEM((count, rows, depth), BF16),
                pltpu.VMEM((rows, wide), F32),
                pltpu.SemaphoreType.DMA((count,)),
            ],
        ),
        out_shape=[jax.ShapeDtypeStruct((rows, wide), F32), jax.ShapeDtypeStruct((rows, wide), BF16)],
        compiler_params=params(30),
        cost_estimate=COST,
        name="ahead",
    )(order, *pieces, weight, pair, ranks, adapters)


def close_kernel(here, back, fwd, across, ranks, adapters, out):
    rank = adapters.shape[1]
    width = out.shape[1]
    value = here[...].astype(F32) + back[...].astype(F32) + fwd[...].astype(F32) + across[...].astype(F32)
    low = jnp.dot(ranks[:, rank:], adapters[0, :, :width], preferred_element_type=F32)
    out[...] = (value + SCALE * low).astype(BF16)


def add_kernel(a0, a1, b0, b1, b2, out_a, out_b):
    out_a[...] = (a0[...].astype(F32) + a1[...].astype(F32)).astype(BF16)
    out_b[...] = (b0[...].astype(F32) + b1[...].astype(F32) + b2[...].astype(F32)).astype(BF16)


def add_both(*terms):
    rows, wide = terms[0].shape
    spec = pl.BlockSpec((rows // 2, wide), lambda i: (i, 0))
    return pl.pallas_call(
        add_kernel,
        grid=(2,),
        in_specs=[spec] * len(terms),
        out_specs=[spec] * 2,
        out_shape=[jax.ShapeDtypeStruct((rows, wide), BF16)] * 2,
        compiler_params=params(WIDE),
        cost_estimate=COST,
        name="add_both",
    )(*terms)


def one_kernel(a0, a1, out):
    out[...] = (a0[...].astype(F32) + a1[...].astype(F32)).astype(BF16)


def add(*terms):
    rows, wide = terms[0].shape
    spec = pl.BlockSpec((rows // 2, wide), lambda i: (i, 0))
    return pl.pallas_call(
        one_kernel,
        grid=(2,),
        in_specs=[spec] * 2,
        out_specs=spec,
        out_shape=jax.ShapeDtypeStruct((rows, wide), BF16),
        compiler_params=params(WIDE),
        cost_estimate=COST,
        name="add",
    )(*terms)


def plus(*terms):
    total = terms[0].astype(F32)
    for term in terms[1:]:
        total = total + term.astype(F32)
    return total


def shards(tokens, base_weight, adapt_down, adapt_up, cotangent, tenant, adapter_slot):
    member = lax.axis_index("mem").astype(jnp.int32)
    core, y, x = member % 2, (member // 2) % YY, member // (2 * YY)
    rows, feats = tokens.shape
    hidden = cotangent.shape[1]
    both = feats + hidden
    per_group, _, rank = adapt_down.shape
    piece = rank // GRP
    block_rows = rows // BLK

    match = tenant[:, None] == jnp.arange(adapter_slot.shape[0], dtype=jnp.int32)[None, :]
    slots = jnp.sum(jnp.where(match, adapter_slot[None, :], 0), axis=1)

    def block_order(c):
        d = 1 - 2 * c
        steps = ((0, 0), (1, 0), (0, -d), (0, d), (1, -d), (1, d), (0, 2), (1, 2))
        return jnp.stack([((x ^ dx) * YY + (y + dy + YY) % YY) * 2 + c for dx, dy in steps]).astype(jnp.int32)

    order = block_order(core)
    piece_shape = pltpu.HBM((GRP, per_group, piece, both), BF16)
    all_pieces = pl.BlockSpec(piece_shape.shape, lambda i: (0, 0, 0, 0))
    weight = stay(base_weight.reshape(2 * XL * YY, feats, hidden))

    pair_w = stay(send(base_weight, "core", "w_all").reshape(weight.shape))
    t_x = stay(send(tokens, "x", "t_x"))
    t_f = stay(send(tokens, "fwd", "t_f"))
    t_b = stay(send(tokens, "back", "t_b"))
    cot_pair = send(cotangent, "core", "c_cot")
    cut = pl.pallas_call(
        cut_kernel,
        grid=(per_group,),
        in_specs=[
            pl.BlockSpec((1, GRP, piece, feats), lambda b: (b, 0, 0, 0)),
            pl.BlockSpec((1, GRP, piece, hidden), lambda b: (b, 0, 0, 0)),
        ],
        out_specs=pl.BlockSpec((GRP, 1, piece, both), lambda b: (0, b, 0, 0)),
        out_shape=piece_shape,
        compiler_params=params(WIDE),
        cost_estimate=COST,
        name="cut",
    )(
        stay(jnp.swapaxes(adapt_down, 1, 2).reshape(per_group, GRP, piece, feats)),
        stay(adapt_up.reshape(per_group, GRP, piece, hidden)),
    )
    got = exchange(cut)
    got, t_x, t_f, t_b = lax.optimization_barrier((got, t_x, t_f, t_b))

    t_ff = stay(send(t_f, "fwd", "t_ff"))
    t_xf = stay(send(t_x, "fwd", "t_xf"))
    t_xb = stay(send(t_x, "back", "t_xb"))
    picked = pl.pallas_call(
        pick_kernel,
        grid=(1,),
        in_specs=[SMEM, all_pieces],
        out_specs=all_pieces,
        out_shape=piece_shape,
        compiler_params=params(4),
        cost_estimate=COST,
        name="pick",
    )(slots, got)
    own = exchange(picked)
    parts = backward(cotangent, cot_pair, weight, pair_w, order)
    own, parts, t_ff, t_xf, t_xb = lax.optimization_barrier((own, parts, t_ff, t_xf, t_xb))
    g00, g10, g0b, g0f, g1b, g1f, g02, g12 = parts

    r_12 = send(g12, "x", "r_12")
    t_xff = stay(send(t_xf, "fwd", "t_xff"))
    adapters, part = pl.pallas_call(
        rank_kernel,
        grid=(BLK,),
        in_specs=[
            pl.BlockSpec((block_rows, feats), lambda b: (b, 0)),
            pl.BlockSpec((block_rows, hidden), lambda b: (b, 0)),
            pl.BlockSpec((GRP, 1, piece, both), lambda b: (0, b, 0, 0)),
        ],
        out_specs=[
            pl.BlockSpec((1, rank, both), lambda b: (b, 0, 0)),
            pl.BlockSpec((block_rows, 2 * rank), lambda b: (b, 0)),
        ],
        out_shape=[
            jax.ShapeDtypeStruct((BLK, rank, both), BF16),
            jax.ShapeDtypeStruct((rows, 2 * rank), F32),
        ],
        compiler_params=params(6),
        cost_estimate=COST,
        name="rank",
    )(tokens, cotangent, own)
    chip = (part + send(part, "core", "k_core")).astype(BF16)
    two = plus(chip, send(chip, "x", "k_x")).astype(BF16)
    ranks = plus(two, send(two, "fwd", "k_f"), send(two, "back", "k_b"), send(two, "far", "k_far")).astype(BF16)
    ranks, r_12, t_xff = lax.optimization_barrier((ranks, r_12, t_xff))

    grads = pl.pallas_call(
        grad_kernel,
        grid=(BLK,),
        in_specs=[
            pl.BlockSpec((block_rows, feats), lambda b: (b, 0)),
            pl.BlockSpec((block_rows, hidden), lambda b: (b, 0)),
            pl.BlockSpec((block_rows, 2 * rank), lambda b: (b, 0)),
        ],
        out_specs=pl.BlockSpec((GRP, 1, piece, both), lambda b: (0, b, 0, 0)),
        out_shape=piece_shape,
        compiler_params=params(6),
        cost_estimate=COST,
        name="grads",
    )(tokens, cotangent, ranks)
    got = exchange(grads)
    r_1b = send(g1b, "back", "r_1b")
    r_1f = send(g1f, "fwd", "r_1f")
    r_02 = send(add(g02, r_12), "back", "r_02")
    sum_0b, sum_10 = add_both(g0b, r_02, g10, r_1b, r_1f)
    r_0f = send(g0f, "fwd", "r_0f")
    r_0b = send(sum_0b, "back", "r_0b")
    r_10 = send(sum_10, "x", "r_10")
    t_xff, sum_0b, sum_10 = lax.optimization_barrier((t_xff, sum_0b, sum_10))
    pieces = (tokens, t_x, t_f, t_b, t_xf, t_xb, t_ff, t_xff)
    own_sum, pair_sum = ahead(pieces, weight, pair_w, ranks, adapters, order)
    got, own_sum, pair_sum, r_0b, r_0f, r_10 = lax.optimization_barrier((got, own_sum, pair_sum, r_0b, r_0f, r_10))

    totals = pl.pallas_call(
        total_kernel,
        grid=(1,),
        in_specs=[SMEM, all_pieces],
        out_specs=all_pieces,
        out_shape=piece_shape,
        scratch_shapes=[pltpu.VMEM((GRP * per_group, piece, both), F32)],
        compiler_params=params(6),
        cost_estimate=COST,
        name="total",
    )(slots, got)
    final = exchange(totals)
    mixed = (own_sum + send(pair_sum, "core", "c_sum").astype(F32)).astype(BF16)
    step = pl.BlockSpec((block_rows, feats), lambda b: (b, 0))
    token_gradient = pl.pallas_call(
        close_kernel,
        grid=(BLK,),
        in_specs=[
            step,
            step,
            step,
            step,
            pl.BlockSpec((block_rows, 2 * rank), lambda b: (b, 0)),
            pl.BlockSpec((1, rank, both), lambda b: (b, 0, 0)),
        ],
        out_specs=pl.BlockSpec((block_rows, feats), lambda b: (b, 0)),
        out_shape=jax.ShapeDtypeStruct((rows, feats), BF16),
        compiler_params=params(WIDE),
        cost_estimate=COST,
        name="close",
    )(g00, r_0b, r_0f, r_10, ranks, adapters)
    final, mixed, token_gradient = lax.optimization_barrier((final, mixed, token_gradient))
    down_grad, up_grad = pl.pallas_call(
        join_kernel,
        grid=(per_group,),
        in_specs=[pl.BlockSpec((GRP, 1, piece, both), lambda b: (0, b, 0, 0))],
        out_specs=[
            pl.BlockSpec((1, GRP, piece, feats), lambda b: (b, 0, 0, 0)),
            pl.BlockSpec((1, GRP, piece, hidden), lambda b: (b, 0, 0, 0)),
        ],
        out_shape=[
            jax.ShapeDtypeStruct((per_group, GRP, piece, feats), BF16),
            jax.ShapeDtypeStruct((per_group, GRP, piece, hidden), BF16),
        ],
        compiler_params=params(4),
        cost_estimate=COST,
        name="join",
    )(final)
    down_grad = jnp.swapaxes(down_grad.reshape(per_group, rank, feats), 1, 2)
    return mixed, token_gradient, down_grad, up_grad.reshape(per_group, rank, hidden)


def solution(mesh):
    in_specs = (
        P("grp", "mem"),
        P(None, "mem"),
        P("grp", "mem", None),
        P("grp", None, "mem"),
        P("grp", "mem"),
        P(),
        P(),
    )
    out_specs = (P("grp", "mem"), P("grp", "mem"), P("grp", "mem", None), P("grp", None, "mem"))
    return jax.shard_map(shards, mesh=mesh, in_specs=in_specs, out_specs=out_specs, check_vma=False)
```

```python
import functools

import jax
import jax.numpy as jnp
from jax import lax
from jax.experimental import pallas as pl
from jax.experimental.pallas import tpu as pltpu
from jax.sharding import PartitionSpec as P

SCALE = 8.0
GRP, XL, YY, CORES = 8, 2, 4, 2
BLK = 4
F32, BF16 = jnp.float32, jnp.bfloat16
VMEM = pl.BlockSpec(memory_space=pltpu.VMEM)
SMEM = pl.BlockSpec(memory_space=pltpu.SMEM)
HBM = pl.BlockSpec(memory_space=pltpu.HBM)
ANY = pl.BlockSpec(memory_space=pl.ANY)
WIDE = 56
COST = pl.CostEstimate(flops=1, bytes_accessed=1, transcendentals=0)
NT = (((1,), (1,)), ((), ()))
TN = (((0,), (0,)), ((), ()))


def mem_perm(move):
    pairs = []
    for x in range(XL):
        for y in range(YY):
            for c in range(CORES):
                tx, ty, tc = move(x, y, c)
                pairs.append(((x * YY + y) * CORES + c, (tx * YY + ty % YY) * CORES + tc))
    return pairs


def way(c):
    return 1 - 2 * c


MOVES = {
    "core": mem_perm(lambda x, y, c: (x, y, 1 - c)),
    "x": mem_perm(lambda x, y, c: (1 - x, y, c)),
    "fwd": mem_perm(lambda x, y, c: (x, y + way(c), c)),
    "back": mem_perm(lambda x, y, c: (x, y - way(c), c)),
    "far": mem_perm(lambda x, y, c: (x, y + 2, c)),
}


def send(value, move, name):
    with jax.named_scope(name):
        return lax.ppermute(value, "mem", MOVES[move])


def stay(value):
    return pltpu.with_memory_space_constraint(value, pltpu.HBM)


def exchange(pieces):
    return lax.all_to_all(pieces, "grp", 0, 0, tiled=True)


def params(mib):
    return pltpu.CompilerParams(vmem_limit_bytes=mib * 1024 * 1024)


def cut_kernel(down, up, out):
    width = down.shape[-1]
    for b in range(down.shape[0]):
        out[:, b, :, :width] = down[b]
        out[:, b, :, width:] = up[b]


def pick_kernel(slots, got, out):
    for i in range(GRP):
        for b in range(BLK):
            slot = slots[BLK * i + b]
            out[i, b] = got[slot // BLK, slot % BLK]


def rank_kernel(tokens, cot, got, adapters, part):
    width = tokens.shape[1]
    rank = adapters.shape[1]
    whole = jnp.concatenate([got[i, 0].astype(F32) for i in range(GRP)], axis=0).astype(BF16)
    adapters[0] = whole
    part[:, :rank] = lax.dot_general(tokens[...], whole[:, :width], NT, preferred_element_type=F32)
    part[:, rank:] = lax.dot_general(cot[...], whole[:, width:], NT, preferred_element_type=F32)


def grad_kernel(tokens, cot, ranks, out):
    width = tokens.shape[1]
    rows = tokens.shape[0]
    rank = ranks.shape[1] // 2
    piece = rank // GRP
    factor = SCALE / rows
    both = ranks[...]
    down = lax.dot_general(both[:, rank:], tokens[...], TN, preferred_element_type=F32) * factor
    up = lax.dot_general(both[:, :rank], cot[...], TN, preferred_element_type=F32) * factor
    for i in range(GRP):
        part = slice(i * piece, (i + 1) * piece)
        out[i, 0, :, :width] = down[part].astype(BF16)
        out[i, 0, :, width:] = up[part].astype(BF16)


def total_kernel(slots, got, out, total):
    total[...] = jnp.zeros_like(total)
    for i in range(GRP):
        for b in range(BLK):
            slot = slots[BLK * i + b]
            total[slot] = total[slot] + got[i, b].astype(F32)
    for i in range(GRP):
        out[i] = total[BLK * i : BLK * (i + 1)].astype(BF16)


def join_kernel(got, down, up):
    width = down.shape[-1]
    down[0] = got[:, 0, :, :width]
    up[0] = got[:, 0, :, width:]


def back_kernel(count, order, cot, cot_pair, own, pair, *refs):
    outs, (ready, out_sems) = refs[:count], refs[count:]
    i = pl.program_id(0)
    copies = [pltpu.make_async_copy(ready.at[k % 2], outs[k], out_sems.at[k % 2]) for k in range(count)]
    for k in range(2, count):

        @pl.when(i == k)
        def _():
            copies[k - 2].wait()

    value = lax.dot_general(cot[...], own[0], NT, preferred_element_type=F32)
    value += lax.dot_general(cot_pair[...], pair[0], NT, preferred_element_type=F32)
    ready[lax.rem(i, 2)] = value.astype(BF16)
    for k in range(count):

        @pl.when(i == k)
        def _():
            copies[k].start()

    @pl.when(i == count - 1)
    def _():
        copies[-2].wait()
        copies[-1].wait()


def backward(cot, cot_pair, weight, pair, order):
    count = order.shape[0]
    rows, wide = cot.shape
    depth = weight.shape[1]
    whole = pl.BlockSpec((rows, wide), lambda i, order: (0, 0))
    block = pl.BlockSpec((1, depth, wide), lambda i, order: (order[i], 0, 0))
    return pl.pallas_call(
        functools.partial(back_kernel, count),
        grid_spec=pltpu.PrefetchScalarGridSpec(
            num_scalar_prefetch=1,
            grid=(count,),
            in_specs=[whole, whole, block, block],
            out_specs=[HBM] * count,
            scratch_shapes=[pltpu.VMEM((2, rows, depth), BF16), pltpu.SemaphoreType.DMA((2,))],
        ),
        out_shape=[pltpu.HBM((rows, depth), BF16)] * count,
        compiler_params=params(30),
        cost_estimate=COST,
        name="backward",
    )(order, cot, cot_pair, weight, pair)


def ahead_kernel(count, order, *refs):
    pieces, weight, (*start, out, held, total, sems) = refs[:count], refs[count], refs[count + 1 :]
    i = pl.program_id(0)
    copies = [pltpu.make_async_copy(s, held.at[k], sems.at[k]) for k, s in enumerate(pieces)]

    @pl.when(i == 0)
    def _():
        for copy in copies:
            copy.start()
        if start:
            ranks, adapters, other = start
            rank = adapters.shape[1]
            rows = ranks.shape[0] // BLK
            width = adapters.shape[2] - out.shape[1]
            for b in range(BLK):
                span = slice(b * rows, (b + 1) * rows)
                low = jnp.dot(ranks[span, :rank], adapters[b, :, width:], preferred_element_type=F32)
                total[span, :] = SCALE * low + other[span, :].astype(F32)
        else:
            total[...] = jnp.zeros_like(total)

    for k in range(count):

        @pl.when(i == k)
        def _():
            copies[k].wait()

    total[...] += jnp.dot(held[i], weight[0], preferred_element_type=F32)

    @pl.when(i == count - 1)
    def _():
        out[...] = total[...].astype(BF16)


def ahead(pieces, weight, order, start=()):
    count = len(pieces)
    rows, depth = pieces[0].shape
    wide = weight.shape[2]
    starts = [pl.BlockSpec(v.shape, lambda i, order, n=v.ndim: (0,) * n) for v in start]
    return pl.pallas_call(
        functools.partial(ahead_kernel, count),
        grid_spec=pltpu.PrefetchScalarGridSpec(
            num_scalar_prefetch=1,
            grid=(count,),
            in_specs=[HBM] * count
            + [pl.BlockSpec((1, depth, wide), lambda i, order: (order[i], 0, 0))]
            + starts,
            out_specs=pl.BlockSpec((rows, wide), lambda i, order: (0, 0)),
            scratch_shapes=[
                pltpu.VMEM((count, rows, depth), BF16),
                pltpu.VMEM((rows, wide), F32),
                pltpu.SemaphoreType.DMA((count,)),
            ],
        ),
        out_shape=jax.ShapeDtypeStruct((rows, wide), BF16),
        compiler_params=params(24),
        cost_estimate=COST,
        name="ahead_own" if start else "ahead_pair",
    )(order, *pieces, weight, *start)


def close_kernel(here, back, fwd, across, ranks, adapters, out):
    rank = adapters.shape[1]
    rows, width = out.shape
    each = rows // adapters.shape[0]
    value = here[...].astype(F32) + back[...].astype(F32) + fwd[...].astype(F32) + across[...].astype(F32)
    for b in range(adapters.shape[0]):
        span = slice(b * each, (b + 1) * each)
        low = jnp.dot(ranks[span, rank:], adapters[b, :, :width], preferred_element_type=F32)
        out[span, :] = (value[span, :] + SCALE * low).astype(BF16)


def add_kernel(a0, a1, b0, b1, b2, out_a, out_b):
    out_a[...] = (a0[...].astype(F32) + a1[...].astype(F32)).astype(BF16)
    out_b[...] = (b0[...].astype(F32) + b1[...].astype(F32) + b2[...].astype(F32)).astype(BF16)


def add_both(*terms):
    rows, wide = terms[0].shape
    spec = pl.BlockSpec((rows // 2, wide), lambda i: (i, 0))
    return pl.pallas_call(
        add_kernel,
        grid=(2,),
        in_specs=[spec] * len(terms),
        out_specs=[spec] * 2,
        out_shape=[jax.ShapeDtypeStruct((rows, wide), BF16)] * 2,
        compiler_params=params(WIDE),
        cost_estimate=COST,
        name="add_both",
    )(*terms)


def one_kernel(a0, a1, out):
    out[...] = (a0[...].astype(F32) + a1[...].astype(F32)).astype(BF16)


def add(*terms):
    rows, wide = terms[0].shape
    spec = pl.BlockSpec((rows // 2, wide), lambda i: (i, 0))
    return pl.pallas_call(
        one_kernel,
        grid=(2,),
        in_specs=[spec] * 2,
        out_specs=spec,
        out_shape=jax.ShapeDtypeStruct((rows, wide), BF16),
        compiler_params=params(WIDE),
        cost_estimate=COST,
        name="add",
    )(*terms)


def plus(*terms):
    total = terms[0].astype(F32)
    for term in terms[1:]:
        total = total + term.astype(F32)
    return total


def shards(tokens, base_weight, adapt_down, adapt_up, cotangent, tenant, adapter_slot):
    member = lax.axis_index("mem").astype(jnp.int32)
    core, y, x = member % 2, (member // 2) % YY, member // (2 * YY)
    rows, feats = tokens.shape
    hidden = cotangent.shape[1]
    both = feats + hidden
    per_group, _, rank = adapt_down.shape
    piece = rank // GRP
    block_rows = rows // BLK

    match = tenant[:, None] == jnp.arange(adapter_slot.shape[0], dtype=jnp.int32)[None, :]
    slots = jnp.sum(jnp.where(match, adapter_slot[None, :], 0), axis=1)

    def block_order(c):
        d = 1 - 2 * c
        steps = ((0, 0), (1, 0), (0, -d), (0, d), (1, -d), (1, d), (0, 2), (1, 2))
        return jnp.stack([((x ^ dx) * YY + (y + dy + YY) % YY) * 2 + c for dx, dy in steps]).astype(jnp.int32)

    order = block_order(core)
    piece_shape = pltpu.HBM((GRP, per_group, piece, both), BF16)
    all_pieces = pl.BlockSpec(piece_shape.shape, lambda i: (0, 0, 0, 0))
    weight = stay(base_weight.reshape(2 * XL * YY, feats, hidden))

    pair_w = stay(send(base_weight, "core", "w_all").reshape(weight.shape))
    t_x = stay(send(tokens, "x", "t_x"))
    t_f = stay(send(tokens, "fwd", "t_f"))
    t_b = stay(send(tokens, "back", "t_b"))
    cot_pair = send(cotangent, "core", "c_cot")
    cut = pl.pallas_call(
        cut_kernel,
        grid=(per_group // 2,),
        in_specs=[
            pl.BlockSpec((2, GRP, piece, feats), lambda b: (b, 0, 0, 0)),
            pl.BlockSpec((2, GRP, piece, hidden), lambda b: (b, 0, 0, 0)),
        ],
        out_specs=pl.BlockSpec((GRP, 2, piece, both), lambda b: (0, b, 0, 0)),
        out_shape=piece_shape,
        compiler_params=params(WIDE),
        cost_estimate=COST,
        name="cut",
    )(
        stay(jnp.swapaxes(adapt_down, 1, 2).reshape(per_group, GRP, piece, feats)),
        stay(adapt_up.reshape(per_group, GRP, piece, hidden)),
    )
    got = exchange(cut)
    got, t_x, t_f, t_b = lax.optimization_barrier((got, t_x, t_f, t_b))

    t_ff = stay(send(t_f, "fwd", "t_ff"))
    t_xf = stay(send(t_x, "fwd", "t_xf"))
    t_xb = stay(send(t_x, "back", "t_xb"))
    picked = pl.pallas_call(
        pick_kernel,
        grid=(1,),
        in_specs=[SMEM, all_pieces],
        out_specs=all_pieces,
        out_shape=piece_shape,
        compiler_params=params(4),
        cost_estimate=COST,
        name="pick",
    )(slots, got)
    own = exchange(picked)
    parts = backward(cotangent, cot_pair, weight, pair_w, order)
    own, parts, t_ff, t_xf, t_xb = lax.optimization_barrier((own, parts, t_ff, t_xf, t_xb))
    g00, g10, g0b, g0f, g1b, g1f, g02, g12 = parts

    r_12 = send(g12, "x", "r_12")
    t_xff = stay(send(t_xf, "fwd", "t_xff"))
    adapters, part = pl.pallas_call(
        rank_kernel,
        grid=(BLK,),
        in_specs=[
            pl.BlockSpec((block_rows, feats), lambda b: (b, 0)),
            pl.BlockSpec((block_rows, hidden), lambda b: (b, 0)),
            pl.BlockSpec((GRP, 1, piece, both), lambda b: (0, b, 0, 0)),
        ],
        out_specs=[
            pl.BlockSpec((1, rank, both), lambda b: (b, 0, 0)),
            pl.BlockSpec((block_rows, 2 * rank), lambda b: (b, 0)),
        ],
        out_shape=[
            jax.ShapeDtypeStruct((BLK, rank, both), BF16),
            jax.ShapeDtypeStruct((rows, 2 * rank), F32),
        ],
        compiler_params=params(6),
        cost_estimate=COST,
        name="rank",
    )(tokens, cotangent, own)
    chip = (part + send(part, "core", "k_core")).astype(BF16)
    two = plus(chip, send(chip, "x", "k_x")).astype(BF16)
    ranks = plus(two, send(two, "fwd", "k_f"), send(two, "back", "k_b"), send(two, "far", "k_far")).astype(BF16)
    ranks, r_12, t_xff = lax.optimization_barrier((ranks, r_12, t_xff))

    grads = pl.pallas_call(
        grad_kernel,
        grid=(BLK,),
        in_specs=[
            pl.BlockSpec((block_rows, feats), lambda b: (b, 0)),
            pl.BlockSpec((block_rows, hidden), lambda b: (b, 0)),
            pl.BlockSpec((block_rows, 2 * rank), lambda b: (b, 0)),
        ],
        out_specs=pl.BlockSpec((GRP, 1, piece, both), lambda b: (0, b, 0, 0)),
        out_shape=piece_shape,
        compiler_params=params(6),
        cost_estimate=COST,
        name="grads",
    )(tokens, cotangent, ranks)
    got = exchange(grads)
    r_1b = send(g1b, "back", "r_1b")
    r_1f = send(g1f, "fwd", "r_1f")
    r_02 = send(add(g02, r_12), "back", "r_02")
    sum_0b, sum_10 = add_both(g0b, r_02, g10, r_1b, r_1f)
    r_0f = send(g0f, "fwd", "r_0f")
    r_0b = send(sum_0b, "back", "r_0b")
    r_10 = send(sum_10, "x", "r_10")
    t_xff, sum_0b, sum_10 = lax.optimization_barrier((t_xff, sum_0b, sum_10))
    pieces = (tokens, t_x, t_f, t_b, t_xf, t_xb, t_ff, t_xff)
    pair_sum = ahead(pieces, pair_w, order)
    got, pair_sum, r_0b, r_0f, r_10 = lax.optimization_barrier((got, pair_sum, r_0b, r_0f, r_10))

    totals = pl.pallas_call(
        total_kernel,
        grid=(1,),
        in_specs=[SMEM, all_pieces],
        out_specs=all_pieces,
        out_shape=piece_shape,
        scratch_shapes=[pltpu.VMEM((GRP * per_group, piece, both), F32)],
        compiler_params=params(6),
        cost_estimate=COST,
        name="total",
    )(slots, got)
    final = exchange(totals)
    mixed = ahead(pieces, weight, order, (ranks, adapters, send(pair_sum, "core", "c_sum")))
    step = pl.BlockSpec((2 * block_rows, feats), lambda b: (b, 0))
    token_gradient = pl.pallas_call(
        close_kernel,
        grid=(BLK // 2,),
        in_specs=[
            step,
            step,
            step,
            step,
            pl.BlockSpec((2 * block_rows, 2 * rank), lambda b: (b, 0)),
            pl.BlockSpec((2, rank, both), lambda b: (b, 0, 0)),
        ],
        out_specs=pl.BlockSpec((2 * block_rows, feats), lambda b: (b, 0)),
        out_shape=jax.ShapeDtypeStruct((rows, feats), BF16),
        compiler_params=params(40),
        cost_estimate=COST,
        name="close",
    )(g00, r_0b, r_0f, r_10, ranks, adapters)
    final, mixed, token_gradient = lax.optimization_barrier((final, mixed, token_gradient))
    down_grad, up_grad = pl.pallas_call(
        join_kernel,
        grid=(per_group,),
        in_specs=[pl.BlockSpec((GRP, 1, piece, both), lambda b: (0, b, 0, 0))],
        out_specs=[
            pl.BlockSpec((1, GRP, piece, feats), lambda b: (b, 0, 0, 0)),
            pl.BlockSpec((1, GRP, piece, hidden), lambda b: (b, 0, 0, 0)),
        ],
        out_shape=[
            jax.ShapeDtypeStruct((per_group, GRP, piece, feats), BF16),
            jax.ShapeDtypeStruct((per_group, GRP, piece, hidden), BF16),
        ],
        compiler_params=params(4),
        cost_estimate=COST,
        name="join",
    )(final)
    down_grad = jnp.swapaxes(down_grad.reshape(per_group, rank, feats), 1, 2)
    return mixed, token_gradient, down_grad, up_grad.reshape(per_group, rank, hidden)


def solution(mesh):
    in_specs = (
        P("grp", "mem"),
        P(None, "mem"),
        P("grp", "mem", None),
        P("grp", None, "mem"),
        P("grp", "mem"),
        P(),
        P(),
    )
    out_specs = (P("grp", "mem"), P("grp", "mem"), P("grp", "mem", None), P("grp", None, "mem"))
    return jax.shard_map(shards, mesh=mesh, in_specs=in_specs, out_specs=out_specs, check_vma=False)
```
